512 devices in a mesh: dp: 64 (over y, z_lo, core), mp: 8 (over x, z_hi).
Axes of the slice: x: 4, y: 4, z: 16 (z_hi: 2, z_lo: 8; z = z_hi * 8 + z_lo), core: 2. Of those that a mesh axis runs over, the one named last changes fastest.
Arguments:
- activations: bfloat16 [65536, 8192], P('dp', 'mp'), may hold values from -400 to 400, as said below
- gradient: bfloat16 [8192, 8192], P('mp', 'dp'), may hold values from -250 to 250
- out_scale: float32 [8192], P('dp'), may hold values from 0.3 to 3
Outputs:
- update: bfloat16 [8192, 8192], P('mp', 'dp')
The draws below stay inside these ranges and needn't reach their ends.
Inputs may be any that keep to these rules, and one draw needn't show every extreme that they name: activations entering the projection.
All inputs are finite; a program needn't handle non-finite values. Where the reference program divides by a largest or mean magnitude, that divisor is 1e-20 or more.
Results may differ from the reference program's by a relative error of at most 0.001.
Values sent between devices are 32-bit elements; how exact they have to be, the bound alone decides.
No kernel may reach another device: no remote copies, remote signals or barrier semaphores. Data moves between devices by JAX's collectives and lax.ppermute only.
A program may use at most 64 MiB of HBM per device.

```python
import math
import jax
import jax.numpy as jnp
from jax import lax

D = 8192
BLOCK = 1024
TOK_DEV = 1024
TOKENS = 65536
ROWS = 16


def clipped_normal(key, shape):
    return jnp.clip(jax.random.normal(key, shape, jnp.float32), -4.0, 4.0)


def log_spread(key, shape, lower, upper):
    return jnp.exp(jax.random.uniform(key, shape, jnp.float32, math.log(lower), math.log(upper)))


def draw_activations(key, part):
    key = jax.random.fold_in(key, 11)
    keys = jax.random.split(key, 6)
    column_scale = log_spread(keys[1], (1, D), 0.5, 5.0)
    shared = clipped_normal(keys[5], (TOKENS, 1))
    loading = 0.5 * jnp.clip(2.0 - column_scale, 0.0, 1.0)
    noise = clipped_normal(keys[0], (TOKENS, D))
    blended = noise + 0.6 * jnp.roll(noise, -1, axis=1) + loading * shared
    pairing = jax.random.permutation(keys[2], TOKENS // TOK_DEV)
    owner_of_token = pairing[jnp.arange(TOKENS) // TOK_DEV]
    sub_block = jnp.arange(D) % BLOCK // ROWS
    spike = jnp.where(owner_of_token[:, None] == sub_block[None, :], 2.5, 1.0)
    return (blended * column_scale * spike).astype(jnp.bfloat16)


def draw_gradient(key, part):
    key = jax.random.fold_in(key, 23)
    keys = jax.random.split(key, 1)
    noise = clipped_normal(keys[0], (D, D))
    row_ramp = 1.0 + jnp.arange(D, dtype=jnp.float32) / (D - 1)
    column_ramp = 1.0 + 2.0 * jnp.arange(D, dtype=jnp.float32) / (D - 1)
    return (6.0 * noise * row_ramp[:, None] * column_ramp[None, :]).astype(jnp.bfloat16)


def level_of(stream_key, dims, shards, low, high):
    def one(dim, shards_of):
        draws = jax.random.uniform(jax.random.fold_in(jax.random.fold_in(stream_key, 6), dim), (shards_of,), jnp.float32, low / len(shards), high / len(shards))
        return jnp.repeat(jnp.exp(draws), dims[dim] // shards_of).reshape((-1,) + (1,) * (len(dims) - dim - 1))

    gain = one(*shards[0])
    for cut in shards[1:]:
        gain = gain * one(*cut)
    return gain


def setup_inputs(seed: int = 0) -> dict:
    seeds = jax.random.split(jax.random.key(seed), 4)
    return {
        "activations": draw_activations(jax.random.fold_in(seeds[3], 71), 0),
        "gradient": draw_gradient(jax.random.fold_in(seeds[3], 71), 0),
        "out_scale": jnp.clip(jnp.exp(math.log(3.0) - 2.3025851 * jax.random.uniform(seeds[2], (D,), jnp.float32) ** level_of(seeds[2], (D,), ((0, 64),), -0.2, 0.2)), 0.3, 3.0),
    }


damping = 0.1
kl_bound = 2.0

def reference(activations, gradient, out_scale):
    highest = lax.Precision.HIGHEST
    identity = jnp.eye(BLOCK, dtype=jnp.float32)
    results = []
    for block_index in range(D // BLOCK):
        columns = activations[:, block_index * BLOCK:(block_index + 1) * BLOCK]
        factor = jnp.dot(columns.T, columns, preferred_element_type=jnp.float32) / TOKENS + damping * identity
        inv_bound = 1.0 / jnp.max(lax.optimization_barrier(jnp.sum(jnp.abs(factor), axis=1)))
        first = 2.0 * inv_bound * identity - inv_bound * inv_bound * factor
        product = jnp.dot(jnp.dot(first, factor, precision=highest), first, precision=highest)
        second = 2.0 * first - product
        rows_grad = gradient[block_index * BLOCK:(block_index + 1) * BLOCK].astype(jnp.float32)
        results.append(jnp.dot(second, rows_grad, precision=highest))
    scaled = jnp.concatenate(results, axis=0) * out_scale[None, :]
    alignment = jnp.sum(scaled * gradient.astype(jnp.float32)) / (D * D)
    clip_factor = jnp.minimum(1.0, jnp.sqrt(kl_bound / alignment))
    return (scaled * clip_factor).astype(jnp.bfloat16)
```

```python
import functools

import jax
import jax.numpy as jnp
from jax import lax
from jax.experimental import pallas as pl
from jax.experimental.pallas import tpu as pltpu
from jax.sharding import Mesh, PartitionSpec as P

D = 8192
BLOCK = 1024
TILE = 128
HALF = 512
COLS = 128
TOKENS = 65536
SHARE = 18 * TILE

damping = 0.1
kl_bound = 2.0

AXES = ("y", "zb", "zq", "core", "x", "zh")
SIZES = (4, 2, 4, 2, 4, 2)
DP = AXES[:4]
MP = AXES[4:]

f32 = jnp.float32
bf16 = jnp.bfloat16


def gram_kernel(share_ref, own_ref, other_ref, out_ref):
    share = share_ref[0]

    def product(lhs, rhs):
        return lax.dot_general(
            lhs, rhs, (((0,), (0,)), ((), ())), preferred_element_type=f32
        )

    own = own_ref[...]
    other = other_ref[...]
    for pair in range(2):
        lhs = own[:, pair * 256 : (pair + 1) * 256]
        if pair == 0:
            wide = jnp.concatenate([own, other[:, :256]], axis=1)
        else:
            wide = jnp.concatenate([own[:, 256:], other], axis=1)
        strip = product(lhs, wide)
        for i in range(2):
            rows = strip[i * TILE : (i + 1) * TILE]
            for d in range(4):
                k = (pair * 2 + i) * 4 + d
                out_ref[k * TILE : (k + 1) * TILE, :] = rows[
                    :, (i + d) * TILE : (i + d + 1) * TILE
                ]

            @pl.when(share == pair)
            def _():
                k = 16 + i
                out_ref[k * TILE : (k + 1) * TILE, :] = rows[
                    :, (i + 4) * TILE : (i + 5) * TILE
                ]


def gram(share, activations):
    tokens = activations.shape[0]
    return pl.pallas_call(
        gram_kernel,
        out_shape=jax.ShapeDtypeStruct((SHARE, TILE), f32),
        grid_spec=pltpu.PrefetchScalarGridSpec(
            num_scalar_prefetch=1,
            grid=(1,),
            in_specs=[
                pl.BlockSpec((tokens, HALF), lambda g, s: (0, s[0])),
                pl.BlockSpec((tokens, HALF), lambda g, s: (0, 1 - s[0])),
            ],
            out_specs=pl.BlockSpec((SHARE, TILE), lambda g, s: (0, 0)),
        ),
        compiler_params=pltpu.CompilerParams(vmem_limit_bytes=24 * 2**20),
        cost_estimate=pl.CostEstimate(
            flops=2 * tokens * 512 * 768, bytes_accessed=3 * 2**20, transcendentals=0
        ),
        name="gram",
    )(share, activations, activations)


def precondition_kernel(
    share_ref,
    own_ref,
    other_ref,
    grad_lo_ref,
    grad_hi_ref,
    scale_ref,
    scaled_lo_ref,
    scaled_hi_ref,
    align_ref,
    high_ref,
    low_ref,
    sums_ref,
):
    share = share_ref[0]
    eye = lax.broadcasted_iota(jnp.int32, (TILE, TILE), 0) == lax.broadcasted_iota(
        jnp.int32, (TILE, TILE), 1
    )
    sums_ref[...] = jnp.zeros_like(sums_ref)

    def put(tile, i, j):
        high = tile.astype(bf16)
        low = (tile - high.astype(f32)).astype(bf16)
        at = (slice(i * TILE, (i + 1) * TILE), slice(j * TILE, (j + 1) * TILE))
        high_ref[at] = high
        low_ref[at] = low
        part = jnp.abs(tile).reshape(16, 8, TILE)
        sums_ref[:, j * TILE : (j + 1) * TILE] += jnp.sum(part, axis=0)

    def place(ref, k, i, j):
        tile = ref[k * TILE : (k + 1) * TILE, :] * (1.0 / TOKENS)
        if i == j:
            put(tile + jnp.where(eye, damping, 0.0), i, j)
        else:
            put(tile, i, j)
            put(tile.T, j, i)

    for base, ref in ((0, own_ref), (4, other_ref)):
        for i in range(4):
            for d in range(4):
                place(ref, i * 4 + d, base + i, (base + i + d) % 8)
    for core in range(2):

        @pl.when(share == core)
        def _():
            for i in range(2):
                row = 2 * core + i
                place(own_ref, 16 + i, row, row + 4)
                row = 2 * (1 - core) + i
                place(other_ref, 16 + i, row + 4, row)

    bound = 1.0 / jnp.max(jnp.sum(sums_ref[...], axis=0, keepdims=True), axis=1, keepdims=True)
    bound2 = bound * bound
    high = high_ref[...]
    low = low_ref[...]

    def dot(a, b):
        return jnp.dot(a, b, preferred_element_type=f32)

    def times(v):
        v_high = v.astype(bf16)
        v_low = (v - v_high.astype(f32)).astype(bf16)
        both = dot(high, jnp.concatenate([v_high, v_low], axis=1))
        return both[:, :COLS] + (both[:, COLS:] + dot(low, v_high))

    grad16 = jnp.concatenate([grad_lo_ref[...], grad_hi_ref[...]], axis=0)
    grad = grad16.astype(f32)
    u = 2.0 * bound * grad - bound2 * (dot(high, grad16) + dot(low, grad16))
    v = times(u)
    applied = 2.0 * u - (2.0 * bound * v - bound2 * times(v))
    scaled = applied * scale_ref[...]
    scaled_lo_ref[...] = scaled[:HALF]
    scaled_hi_ref[...] = scaled[HALF:]
    local = jnp.sum(scaled * grad, axis=0, keepdims=True)
    align_ref[...] = jnp.broadcast_to(local[None], align_ref.shape)


def precondition(share, own, other, gradient, out_scale, copies):
    whole = lambda g, s: (0, 0)
    half = jax.ShapeDtypeStruct((HALF, COLS), f32)
    return pl.pallas_call(
        precondition_kernel,
        out_shape=(half, half, jax.ShapeDtypeStruct((copies, 1, COLS), f32)),
        grid_spec=pltpu.PrefetchScalarGridSpec(
            num_scalar_prefetch=1,
            grid=(1,),
            in_specs=[
                pl.BlockSpec((SHARE, TILE), whole),
                pl.BlockSpec((SHARE, TILE), whole),
                pl.BlockSpec((HALF, COLS), lambda g, s: (s[0], 0)),
                pl.BlockSpec((HALF, COLS), lambda g, s: (1 - s[0], 0)),
                pl.BlockSpec((1, COLS), whole),
            ],
            out_specs=(
                pl.BlockSpec((HALF, COLS), whole),
                pl.BlockSpec((HALF, COLS), whole),
                pl.BlockSpec((copies, 1, COLS), lambda g, s: (0, 0, 0)),
            ),
            scratch_shapes=[
                pltpu.VMEM((BLOCK, BLOCK), bf16),
                pltpu.VMEM((BLOCK, BLOCK), bf16),
                pltpu.VMEM((8, BLOCK), f32),
            ],
        ),
        compiler_params=pltpu.CompilerParams(vmem_limit_bytes=40 * 2**20),
        cost_estimate=pl.CostEstimate(
            flops=2 * 9 * BLOCK * BLOCK * COLS, bytes_accessed=4 * 2**20, transcendentals=0
        ),
        name="precondition",
    )(share, own, other, gradient, gradient, out_scale.reshape(1, COLS))


def clip_kernel(share_ref, lo_ref, hi_ref, align_ref, out_ref):
    share = share_ref[0]
    lanes = jnp.sum(align_ref[...], axis=0)
    alignment = jnp.sum(lanes, axis=1, keepdims=True) * (1.0 / (D * D))
    factor = jnp.minimum(1.0, jnp.sqrt(kl_bound / alignment))
    for core in range(2):

        @pl.when(share == core)
        def _():
            first, last = (lo_ref, hi_ref) if core == 0 else (hi_ref, lo_ref)
            out_ref[:HALF, :] = (first[...] * factor).astype(bf16)
            out_ref[HALF:, :] = (last[...] * factor).astype(bf16)


def clip(share, lo, hi, align):
    vmem = pl.BlockSpec(memory_space=pltpu.VMEM)
    return pl.pallas_call(
        clip_kernel,
        out_shape=jax.ShapeDtypeStruct((BLOCK, COLS), bf16),
        in_specs=[pl.BlockSpec(memory_space=pltpu.SMEM), vmem, vmem, vmem],
        out_specs=vmem,
        cost_estimate=pl.CostEstimate(
            flops=2 * BLOCK * COLS, bytes_accessed=2**20, transcendentals=0
        ),
        name="clip",
    )(share, lo, hi, align)


def swap_cores(x):
    return lax.ppermute(x, "core", [(0, 1), (1, 0)])


def scatter_sum(x, axes, parts):
    pieces = x.reshape(parts, x.shape[0] // parts, x.shape[1])
    return jnp.sum(lax.all_to_all(pieces, axes, 0, 0), axis=0)


def gather(x, axes, parts):
    copies = jnp.broadcast_to(x[None], (parts, *x.shape))
    return lax.all_to_all(copies, axes, 0, 0).reshape(parts * x.shape[0], x.shape[1])


def on_device(activations, gradient, out_scale):
    core = lax.axis_index("core").astype(jnp.int32)
    mine = core.reshape(1)
    theirs = 1 - mine
    away = swap_cores(gram(theirs, activations))
    chip = gram(mine, activations) + away
    part = scatter_sum(chip, ("y",), 4)
    part = scatter_sum(part, ("zb", "zq"), 8)
    part = gather(part, ("zb", "zq"), 8)
    own = gather(part, ("y",), 4)
    other = swap_cores(own)
    lo, hi, align = precondition(mine, own, other, gradient, out_scale, 32)
    lanes = jnp.sum(lax.all_to_all(align, ("y", "core", "x"), 0, 0), axis=0)
    lanes = jnp.broadcast_to(lanes[None], (16, 1, COLS))
    lanes = lax.all_to_all(lanes, ("zb", "zq", "zh"), 0, 0)
    return clip(mine, lo, hi, lanes)


def solution(mesh):
    fine = Mesh(mesh.devices.reshape(SIZES), AXES)
    return jax.shard_map(
        on_device,
        mesh=fine,
        in_specs=(P(DP, MP), P(MP, DP), P(DP)),
        out_specs=P(MP, DP),
        check_vma=False,
    )
```

```python
import functools

import jax
import jax.numpy as jnp
from jax import lax
from jax.experimental import pallas as pl
from jax.experimental.pallas import tpu as pltpu
from jax.sharding import Mesh, PartitionSpec as P

D = 8192
BLOCK = 1024
TILE = 128
HALF = 512
COLS = 128
TOKENS = 65536
SHARE = 18 * TILE

damping = 0.1
kl_bound = 2.0

AXES = ("y", "z4", "z2", "z1", "core", "x", "z8")
SIZES = (4, 2, 2, 2, 2, 4, 2)
DP = AXES[:5]
MP = AXES[5:]

f32 = jnp.float32
bf16 = jnp.bfloat16


def gram_kernel(share_ref, own_ref, other_ref, out_ref):
    share = share_ref[0]

    def product(lhs, rhs):
        return lax.dot_general(
            lhs, rhs, (((0,), (0,)), ((), ())), preferred_element_type=f32
        )

    own = own_ref[...]
    other = other_ref[...]
    for pair in range(2):
        lhs = own[:, pair * 256 : (pair + 1) * 256]
        if pair == 0:
            wide = jnp.concatenate([own, other[:, :256]], axis=1)
        else:
            wide = jnp.concatenate([own[:, 256:], other], axis=1)
        strip = product(lhs, wide)
        for i in range(2):
            rows = strip[i * TILE : (i + 1) * TILE]
            for d in range(4):
                k = (pair * 2 + i) * 4 + d
                out_ref[k * TILE : (k + 1) * TILE, :] = rows[
                    :, (i + d) * TILE : (i + d + 1) * TILE
                ]

            @pl.when(share == pair)
            def _():
                k = 16 + i
                out_ref[k * TILE : (k + 1) * TILE, :] = rows[
                    :, (i + 4) * TILE : (i + 5) * TILE
                ]


def gram(share, activations):
    tokens = activations.shape[0]
    return pl.pallas_call(
        gram_kernel,
        out_shape=jax.ShapeDtypeStruct((SHARE, TILE), f32),
        grid_spec=pltpu.PrefetchScalarGridSpec(
            num_scalar_prefetch=1,
            grid=(1,),
            in_specs=[
                pl.BlockSpec((tokens, HALF), lambda g, s: (0, s[0])),
                pl.BlockSpec((tokens, HALF), lambda g, s: (0, 1 - s[0])),
            ],
            out_specs=pl.BlockSpec((SHARE, TILE), lambda g, s: (0, 0)),
        ),
        compiler_params=pltpu.CompilerParams(vmem_limit_bytes=24 * 2**20),
        cost_estimate=pl.CostEstimate(
            flops=2 * tokens * 512 * 768, bytes_accessed=3 * 2**20, transcendentals=0
        ),
        name="gram",
    )(share, activations, activations)


def precondition_kernel(
    share_ref,
    own_ref,
    other_ref,
    grad_lo_ref,
    grad_hi_ref,
    scale_ref,
    scaled_ref,
    align_ref,
    high_ref,
    low_ref,
    sums_ref,
):
    share = share_ref[0]
    eye = lax.broadcasted_iota(jnp.int32, (TILE, TILE), 0) == lax.broadcasted_iota(
        jnp.int32, (TILE, TILE), 1
    )
    sums_ref[...] = jnp.zeros_like(sums_ref)

    def put(tile, i, j):
        high = tile.astype(bf16)
        low = (tile - high.astype(f32)).astype(bf16)
        at = (slice(i * TILE, (i + 1) * TILE), slice(j * TILE, (j + 1) * TILE))
        high_ref[at] = high
        low_ref[at] = low
        part = jnp.abs(tile).reshape(16, 8, TILE)
        sums_ref[:, j * TILE : (j + 1) * TILE] += jnp.sum(part, axis=0)

    def place(ref, k, i, j):
        tile = ref[k * TILE : (k + 1) * TILE, :] * (1.0 / TOKENS)
        if i == j:
            put(tile + jnp.where(eye, damping, 0.0), i, j)
        else:
            put(tile, i, j)
            put(tile.T, j, i)

    for base, ref in ((0, own_ref), (4, other_ref)):
        for i in range(4):
            for d in range(4):
                place(ref, i * 4 + d, base + i, (base + i + d) % 8)
    for core in range(2):

        @pl.when(share == core)
        def _():
            for i in range(2):
                row = 2 * core + i
                place(own_ref, 16 + i, row, row + 4)
                row = 2 * (1 - core) + i
                place(other_ref, 16 + i, row + 4, row)

    bound = 1.0 / jnp.max(jnp.sum(sums_ref[...], axis=0, keepdims=True), axis=1, keepdims=True)
    bound2 = bound * bound
    high = high_ref[...]
    low = low_ref[...]

    def dot(a, b):
        return jnp.dot(a, b, preferred_element_type=f32)

    def times(v):
        v_high = v.astype(bf16)
        v_low = (v - v_high.astype(f32)).astype(bf16)
        both = dot(high, jnp.concatenate([v_high, v_low], axis=1))
        return both[:, :COLS] + (both[:, COLS:] + dot(low, v_high))

    grad16 = jnp.concatenate([grad_lo_ref[...], grad_hi_ref[...]], axis=0)
    grad = grad16.astype(f32)
    u = 2.0 * bound * grad - bound2 * (dot(high, grad16) + dot(low, grad16))
    v = times(u)
    applied = 2.0 * u - (2.0 * bound * v - bound2 * times(v))
    scaled = applied * scale_ref[...]
    scaled_ref[pl.ds(pl.multiple_of(share * HALF, HALF), HALF), :] = scaled[:HALF]
    scaled_ref[pl.ds(pl.multiple_of((1 - share) * HALF, HALF), HALF), :] = scaled[HALF:]
    local = jnp.sum(scaled * grad, axis=0, keepdims=True)
    align_ref[...] = jnp.broadcast_to(local[None], align_ref.shape)


def precondition(share, own, other, gradient, out_scale, copies):
    whole = lambda g, s: (0, 0)
    return pl.pallas_call(
        precondition_kernel,
        out_shape=(
            jax.ShapeDtypeStruct((BLOCK, COLS), f32),
            jax.ShapeDtypeStruct((copies, 1, COLS), f32),
        ),
        grid_spec=pltpu.PrefetchScalarGridSpec(
            num_scalar_prefetch=1,
            grid=(1,),
            in_specs=[
                pl.BlockSpec((SHARE, TILE), whole),
                pl.BlockSpec((SHARE, TILE), whole),
                pl.BlockSpec((HALF, COLS), lambda g, s: (s[0], 0)),
                pl.BlockSpec((HALF, COLS), lambda g, s: (1 - s[0], 0)),
                pl.BlockSpec((1, COLS), whole),
            ],
            out_specs=(
                pl.BlockSpec((BLOCK, COLS), whole),
                pl.BlockSpec((copies, 1, COLS), lambda g, s: (0, 0, 0)),
            ),
            scratch_shapes=[
                pltpu.VMEM((BLOCK, BLOCK), bf16),
                pltpu.VMEM((BLOCK, BLOCK), bf16),
                pltpu.VMEM((8, BLOCK), f32),
            ],
        ),
        compiler_params=pltpu.CompilerParams(vmem_limit_bytes=40 * 2**20),
        cost_estimate=pl.CostEstimate(
            flops=2 * 9 * BLOCK * BLOCK * COLS, bytes_accessed=4 * 2**20, transcendentals=0
        ),
        name="precondition",
    )(share, own, other, gradient, gradient, out_scale.reshape(1, COLS))


def clip_kernel(scaled_ref, align_ref, out_ref):
    lanes = jnp.sum(align_ref[...], axis=0)
    alignment = jnp.sum(lanes, axis=1, keepdims=True) * (1.0 / (D * D))
    factor = jnp.minimum(1.0, jnp.sqrt(kl_bound / alignment))
    out_ref[...] = (scaled_ref[...] * factor).astype(bf16)


def clip(scaled, align):
    vmem = pl.BlockSpec(memory_space=pltpu.VMEM)
    return pl.pallas_call(
        clip_kernel,
        out_shape=jax.ShapeDtypeStruct((BLOCK, COLS), bf16),
        in_specs=[vmem, vmem],
        out_specs=vmem,
        cost_estimate=pl.CostEstimate(
            flops=2 * BLOCK * COLS, bytes_accessed=2**20, transcendentals=0
        ),
        name="clip",
    )(scaled, align)


def swap(x, axis):
    return lax.ppermute(x, axis, [(0, 1), (1, 0)])


def scatter_sum(x, axes, parts):
    pieces = x.reshape(parts, x.shape[0] // parts, x.shape[1])
    return jnp.sum(lax.all_to_all(pieces, axes, 0, 0), axis=0)


def gather(x, axes, parts):
    copies = jnp.broadcast_to(x[None], (parts, *x.shape))
    return lax.all_to_all(copies, axes, 0, 0).reshape(parts * x.shape[0], x.shape[1])


def on_device(activations, gradient, out_scale):
    core = lax.axis_index("core").astype(jnp.int32)
    mine = core.reshape(1)
    theirs = 1 - mine
    away = swap(gram(theirs, activations), "core")
    chip = gram(mine, activations) + away
    part = scatter_sum(chip, ("y", "z1"), 8)
    part = part + swap(part, "z2")
    part = part + swap(part, "z4")
    own = gather(part, ("y", "z1"), 8)
    other = swap(own, "core")
    scaled, align = precondition(mine, own, other, gradient, out_scale, 32)
    lanes = jnp.sum(lax.all_to_all(align, ("y", "core", "x"), 0, 0), axis=0)
    lanes = jnp.broadcast_to(lanes[None], (16, 1, COLS))
    lanes = lax.all_to_all(lanes, ("z4", "z2", "z1", "z8"), 0, 0)
    return clip(scaled, lanes)


def solution(mesh):
    fine = Mesh(mesh.devices.reshape(SIZES), AXES)
    return jax.shard_map(
        on_device,
        mesh=fine,
        in_specs=(P(DP, MP), P(MP, DP), P(DP)),
        out_specs=P(MP, DP),
        check_vma=False,
    )
```

```python
import functools

import jax
import jax.numpy as jnp
from jax import lax
from jax.experimental import pallas as pl
from jax.experimental.pallas import tpu as pltpu
from jax.sharding import Mesh, PartitionSpec as P

D = 8192
BLOCK = 1024
TILE = 128
HALF = 512
COLS = 128
TOKENS = 65536
DIAGONALS = 16 * TILE
SHARE = DIAGONALS + 64

damping = 0.1
kl_bound = 2.0

AXES = ("y", "z4", "z2", "z1", "core", "x", "z8")
SIZES = (4, 2, 2, 2, 2, 4, 2)
DP = AXES[:5]
MP = AXES[5:]

f32 = jnp.float32
bf16 = jnp.bfloat16


def row_and_column():
    shape = (TILE, TILE)
    return lax.broadcasted_iota(jnp.int32, shape, 0), lax.broadcasted_iota(jnp.int32, shape, 1)


def tile_at(ref, k):
    return ref.at[k * TILE : (k + 1) * TILE, :]


def off_diagonal(i, d):
    return 2 + 3 * i + d - 1


def gram_kernel(share_ref, own_ref, other_ref, out_ref):
    share = share_ref[0]
    row, column = row_and_column()

    def product(lhs, rhs):
        return lax.dot_general(
            lhs, rhs, (((0,), (0,)), ((), ())), preferred_element_type=f32
        )

    own = own_ref[...]
    other = other_ref[...]
    out_ref[DIAGONALS:, :] = jnp.zeros((SHARE - DIAGONALS, TILE), f32)
    for pair in range(2):
        lhs = own[:, pair * 256 : (pair + 1) * 256]
        if pair == 0:
            wide = jnp.concatenate([own, other[:, :256]], axis=1)
        else:
            wide = jnp.concatenate([own[:, 256:], other], axis=1)
        strip = product(lhs, wide)

        def part(i, d):
            return strip[i * TILE : (i + 1) * TILE, (i + d) * TILE : (i + d + 1) * TILE]

        second = part(1, 0)
        tile_at(out_ref, pair)[...] = jnp.where(row <= column, part(0, 0), second)
        out_ref[DIAGONALS + pair : DIAGONALS + pair + 1, :] = jnp.sum(
            jnp.where(row == column, second, 0.0), axis=0, keepdims=True
        )
        for i in range(2):
            for d in range(1, 4):
                tile_at(out_ref, off_diagonal(2 * pair + i, d))[...] = part(i, d)

            @pl.when(share == pair)
            def _():
                tile_at(out_ref, 14 + i)[...] = part(i, 4)


def gram(share, activations):
    tokens = activations.shape[0]
    return pl.pallas_call(
        gram_kernel,
        out_shape=jax.ShapeDtypeStruct((SHARE, TILE), f32),
        grid_spec=pltpu.PrefetchScalarGridSpec(
            num_scalar_prefetch=1,
            grid=(1,),
            in_specs=[
                pl.BlockSpec((tokens, HALF), lambda g, s: (0, s[0])),
                pl.BlockSpec((tokens, HALF), lambda g, s: (0, 1 - s[0])),
            ],
            out_specs=pl.BlockSpec((SHARE, TILE), lambda g, s: (0, 0)),
        ),
        compiler_params=pltpu.CompilerParams(vmem_limit_bytes=24 * 2**20),
        cost_estimate=pl.CostEstimate(
            flops=2 * tokens * 512 * 768, bytes_accessed=3 * 2**20, transcendentals=0
        ),
        name="gram",
    )(share, activations, activations)


def precondition_kernel(
    share_ref,
    own_ref,
    other_ref,
    grad_lo_ref,
    grad_hi_ref,
    scale_ref,
    scaled_ref,
    align_ref,
    factor_ref,
    sums_ref,
):
    share = share_ref[0]
    row, column = row_and_column()
    sums_ref[...] = jnp.zeros_like(sums_ref)

    def put(tile, i, j):
        high = tile.astype(bf16)
        low = (tile - high.astype(f32)).astype(bf16)
        rows = slice(i * TILE, (i + 1) * TILE)
        factor_ref[rows, j * TILE : (j + 1) * TILE] = high
        factor_ref[rows, BLOCK + j * TILE : BLOCK + (j + 1) * TILE] = low
        part = jnp.abs(tile).reshape(16, 8, TILE)
        sums_ref[:, j * TILE : (j + 1) * TILE] += jnp.sum(part, axis=0)

    def place(ref, k, i, j):
        tile = tile_at(ref, k)[...] * (1.0 / TOKENS)
        put(tile, i, j)
        put(tile.T, j, i)

    def place_diagonal(ref, pair, base):
        tile = tile_at(ref, pair)[...] * (1.0 / TOKENS)
        turned = tile.T
        diagonal = ref[DIAGONALS + pair : DIAGONALS + pair + 1, :] * (1.0 / TOKENS)
        damped = jnp.where(row == column, damping, 0.0)
        at = base + 2 * pair
        put(jnp.where(row <= column, tile, turned) + damped, at, at)
        rest = jnp.where(row > column, tile, turned)
        put(jnp.where(row == column, diagonal, rest) + damped, at + 1, at + 1)

    for base, ref in ((0, own_ref), (4, other_ref)):
        for pair in range(2):
            place_diagonal(ref, pair, base)
        for i in range(4):
            for d in range(1, 4):
                place(ref, off_diagonal(i, d), base + i, (base + i + d) % 8)
    for core in range(2):

        @pl.when(share == core)
        def _():
            for i in range(2):
                first = 2 * core + i
                place(own_ref, 14 + i, first, first + 4)
                first = 2 * (1 - core) + i
                place(other_ref, 14 + i, first + 4, first)

    bound = 1.0 / jnp.max(jnp.sum(sums_ref[...], axis=0, keepdims=True), axis=1, keepdims=True)
    bound2 = bound * bound

    high = factor_ref[:, :BLOCK]
    low = factor_ref[:, BLOCK:]

    def dot(a, b):
        return jnp.dot(a, b, preferred_element_type=f32)

    def times(v):
        v_high = v.astype(bf16)
        v_low = (v - v_high.astype(f32)).astype(bf16)
        both = dot(jnp.concatenate([v_high, v_low], axis=0), high)
        return both[:COLS] + (both[COLS:] + dot(v_high, low))

    grad = jnp.concatenate([grad_lo_ref[...], grad_hi_ref[...]], axis=0).astype(f32)
    turned = grad.T
    turned16 = turned.astype(bf16)
    u = 2.0 * bound * turned - bound2 * (dot(turned16, high) + dot(turned16, low))
    v = times(u)
    applied = 2.0 * u - (2.0 * bound * v - bound2 * times(v))
    scaled = applied.T * scale_ref[...]
    scaled_ref[pl.ds(pl.multiple_of(share * HALF, HALF), HALF), :] = scaled[:HALF]
    scaled_ref[pl.ds(pl.multiple_of((1 - share) * HALF, HALF), HALF), :] = scaled[HALF:]
    local = jnp.sum(scaled * grad, axis=0, keepdims=True)
    align_ref[...] = jnp.broadcast_to(local[None], align_ref.shape)


def precondition(share, own, other, gradient, out_scale, copies):
    whole = lambda g, s: (0, 0)
    return pl.pallas_call(
        precondition_kernel,
        out_shape=(
            jax.ShapeDtypeStruct((BLOCK, COLS), f32),
            jax.ShapeDtypeStruct((copies, 1, COLS), f32),
        ),
        grid_spec=pltpu.PrefetchScalarGridSpec(
            num_scalar_prefetch=1,
            grid=(1,),
            in_specs=[
                pl.BlockSpec((SHARE, TILE), whole),
                pl.BlockSpec((SHARE, TILE), whole),
                pl.BlockSpec((HALF, COLS), lambda g, s: (s[0], 0)),
                pl.BlockSpec((HALF, COLS), lambda g, s: (1 - s[0], 0)),
                pl.BlockSpec((1, COLS), whole),
            ],
            out_specs=(
                pl.BlockSpec((BLOCK, COLS), whole),
                pl.BlockSpec((copies, 1, COLS), lambda g, s: (0, 0, 0)),
            ),
            scratch_shapes=[
                pltpu.VMEM((BLOCK, 2 * BLOCK), bf16),
                pltpu.VMEM((8, BLOCK), f32),
            ],
        ),
        compiler_params=pltpu.CompilerParams(vmem_limit_bytes=40 * 2**20),
        cost_estimate=pl.CostEstimate(
            flops=2 * 9 * BLOCK * BLOCK * COLS, bytes_accessed=4 * 2**20, transcendentals=0
        ),
        name="precondition",
    )(share, own, other, gradient, gradient, out_scale.reshape(1, COLS))


def clip_kernel(scaled_ref, align_ref, out_ref):
    lanes = jnp.sum(align_ref[...], axis=0)
    alignment = jnp.sum(lanes, axis=1, keepdims=True) * (1.0 / (D * D))
    factor = jnp.minimum(1.0, jnp.sqrt(kl_bound / alignment))
    out_ref[...] = (scaled_ref[...] * factor).astype(bf16)


def clip(scaled, align):
    vmem = pl.BlockSpec(memory_space=pltpu.VMEM)
    return pl.pallas_call(
        clip_kernel,
        out_shape=jax.ShapeDtypeStruct((BLOCK, COLS), bf16),
        in_specs=[vmem, vmem],
        out_specs=vmem,
        compiler_params=pltpu.CompilerParams(vmem_limit_bytes=4 * 2**20),
        cost_estimate=pl.CostEstimate(
            flops=2 * BLOCK * COLS, bytes_accessed=2**20, transcendentals=0
        ),
        name="clip",
    )(scaled, align)


def swap(x, axis):
    return lax.ppermute(x, axis, [(0, 1), (1, 0)])


def scatter_sum(x, axes, parts):
    pieces = x.reshape(parts, x.shape[0] // parts, x.shape[1])
    return jnp.sum(lax.all_to_all(pieces, axes, 0, 0), axis=0)


def gather(x, axes, parts):
    copies = jnp.broadcast_to(x[None], (parts, *x.shape))
    return lax.all_to_all(copies, axes, 0, 0).reshape(parts * x.shape[0], x.shape[1])


def on_device(activations, gradient, out_scale):
    core = lax.axis_index("core").astype(jnp.int32)
    mine = core.reshape(1)
    theirs = 1 - mine
    away = swap(gram(theirs, activations), "core")
    chip = gram(mine, activations) + away
    part = scatter_sum(chip, ("y", "z1"), 8)
    part = part + swap(part, "z2")
    part = part + swap(part, "z4")
    own = gather(part, ("y", "z1"), 8)
    other = swap(own, "core")
    scaled, align = precondition(mine, own, other, gradient, out_scale, 32)
    lanes = jnp.sum(lax.all_to_all(align, ("y", "core", "x"), 0, 0), axis=0)
    lanes = jnp.broadcast_to(lanes[None], (16, 1, COLS))
    lanes = lax.all_to_all(lanes, ("z4", "z2", "z1", "z8"), 0, 0)
    return clip(scaled, lanes)


def solution(mesh):
    fine = Mesh(mesh.devices.reshape(SIZES), AXES)
    return jax.shard_map(
        on_device,
        mesh=fine,
        in_specs=(P(DP, MP), P(MP, DP), P(DP)),
        out_specs=P(MP, DP),
        check_vma=False,
    )
```

```python
import functools

import jax
import jax.numpy as jnp
from jax import lax
from jax.experimental import pallas as pl
from jax.experimental.pallas import tpu as pltpu
from jax.sharding import Mesh, PartitionSpec as P

D = 8192
BLOCK = 1024
TILE = 128
HALF = 512
COLS = 128
TOKENS = 65536
DIAGONALS = 16 * TILE
SHARE = DIAGONALS + 64

damping = 0.1
kl_bound = 2.0

AXES = ("y", "z4", "z2", "z1", "core", "x", "z8")
SIZES = (4, 2, 2, 2, 2, 4, 2)
DP = AXES[:5]
MP = AXES[5:]

f32 = jnp.float32
bf16 = jnp.bfloat16


def row_and_column():
    shape = (TILE, TILE)
    return lax.broadcasted_iota(jnp.int32, shape, 0), lax.broadcasted_iota(jnp.int32, shape, 1)


def tile_at(ref, k):
    return ref.at[k * TILE : (k + 1) * TILE, :]


def off_diagonal(i, d):
    return 2 + 3 * i + d - 1


def gram_kernel(share_ref, own_ref, other_ref, out_ref):
    share = share_ref[0]
    row, column = row_and_column()

    def product(lhs, rhs):
        return lax.dot_general(
            lhs, rhs, (((0,), (0,)), ((), ())), preferred_element_type=f32
        )

    own = own_ref[...]
    other = other_ref[...]
    out_ref[DIAGONALS:, :] = jnp.zeros((SHARE - DIAGONALS, TILE), f32)
    for pair in range(2):
        lhs = own[:, pair * 256 : (pair + 1) * 256]
        if pair == 0:
            wide = jnp.concatenate([own, other[:, :256]], axis=1)
        else:
            wide = jnp.concatenate([own[:, 256:], other], axis=1)
        strip = product(lhs, wide)

        def part(i, d):
            return strip[i * TILE : (i + 1) * TILE, (i + d) * TILE : (i + d + 1) * TILE]

        second = part(1, 0)
        tile_at(out_ref, pair)[...] = jnp.where(row <= column, part(0, 0), second)
        out_ref[DIAGONALS + pair : DIAGONALS + pair + 1, :] = jnp.sum(
            jnp.where(row == column, second, 0.0), axis=0, keepdims=True
        )
        for i in range(2):
            for d in range(1, 4):
                tile_at(out_ref, off_diagonal(2 * pair + i, d))[...] = part(i, d)

            @pl.when(share == pair)
            def _():
                tile_at(out_ref, 14 + i)[...] = part(i, 4)


def gram(share, activations):
    tokens = activations.shape[0]
    return pl.pallas_call(
        gram_kernel,
        out_shape=jax.ShapeDtypeStruct((SHARE, TILE), f32),
        grid_spec=pltpu.PrefetchScalarGridSpec(
            num_scalar_prefetch=1,
            grid=(1,),
            in_specs=[
                pl.BlockSpec((tokens, HALF), lambda g, s: (0, s[0])),
                pl.BlockSpec((tokens, HALF), lambda g, s: (0, 1 - s[0])),
            ],
            out_specs=pl.BlockSpec((SHARE, TILE), lambda g, s: (0, 0)),
        ),
        compiler_params=pltpu.CompilerParams(vmem_limit_bytes=24 * 2**20),
        cost_estimate=pl.CostEstimate(
            flops=2 * tokens * 512 * 768, bytes_accessed=3 * 2**20, transcendentals=0
        ),
        name="gram",
    )(share, activations, activations)


def precondition_kernel(
    share_ref,
    own_ref,
    other_ref,
    grad_lo_ref,
    grad_hi_ref,
    scale_ref,
    scaled_ref,
    align_ref,
    factor_ref,
    sums_ref,
):
    share = share_ref[0]
    row, column = row_and_column()
    sums_ref[...] = jnp.zeros_like(sums_ref)

    def put(tile, i, j):
        high = tile.astype(bf16)
        low = (tile - high.astype(f32)).astype(bf16)
        rows = slice(i * TILE, (i + 1) * TILE)
        factor_ref[rows, j * TILE : (j + 1) * TILE] = high
        factor_ref[rows, BLOCK + j * TILE : BLOCK + (j + 1) * TILE] = low
        part = jnp.abs(tile).reshape(16, 8, TILE)
        sums_ref[:, j * TILE : (j + 1) * TILE] += jnp.sum(part, axis=0)

    def place(ref, k, i, j):
        tile = tile_at(ref, k)[...] * (1.0 / TOKENS)
        put(tile, i, j)
        put(tile.T, j, i)

    def place_diagonal(ref, pair, base):
        tile = tile_at(ref, pair)[...] * (1.0 / TOKENS)
        turned = tile.T
        diagonal = ref[DIAGONALS + pair : DIAGONALS + pair + 1, :] * (1.0 / TOKENS)
        damped = jnp.where(row == column, damping, 0.0)
        at = base + 2 * pair
        put(jnp.where(row <= column, tile, turned) + damped, at, at)
        rest = jnp.where(row > column, tile, turned)
        put(jnp.where(row == column, diagonal, rest) + damped, at + 1, at + 1)

    for base, ref in ((0, own_ref), (4, other_ref)):
        for pair in range(2):
            place_diagonal(ref, pair, base)
        for i in range(4):
            for d in range(1, 4):
                place(ref, off_diagonal(i, d), base + i, (base + i + d) % 8)
    for core in range(2):

        @pl.when(share == core)
        def _():
            for i in range(2):
                first = 2 * core + i
                place(own_ref, 14 + i, first, first + 4)
                first = 2 * (1 - core) + i
                place(other_ref, 14 + i, first + 4, first)

    bound = 1.0 / jnp.max(jnp.sum(sums_ref[...], axis=0, keepdims=True), axis=1, keepdims=True)
    bound2 = bound * bound

    high = factor_ref[:, :BLOCK]
    low = factor_ref[:, BLOCK:]

    def dot(a, b):
        return jnp.dot(a, b, preferred_element_type=f32)

    def times(v):
        v_high = v.astype(bf16)
        v_low = (v - v_high.astype(f32)).astype(bf16)
        both = dot(jnp.concatenate([v_high, v_low], axis=0), high)
        return both[:COLS] + (both[COLS:] + dot(v_high, low))

    grad = jnp.concatenate([grad_lo_ref[...], grad_hi_ref[...]], axis=0).astype(f32)
    turned = grad.T
    turned16 = turned.astype(bf16)
    u = 2.0 * bound * turned - bound2 * (dot(turned16, high) + dot(turned16, low))
    v = times(u)
    applied = 2.0 * u - (2.0 * bound * v - bound2 * times(v))
    scaled = applied.T * scale_ref[...]
    scaled_ref[pl.ds(pl.multiple_of(share * HALF, HALF), HALF), :] = scaled[:HALF]
    scaled_ref[pl.ds(pl.multiple_of((1 - share) * HALF, HALF), HALF), :] = scaled[HALF:]
    local = jnp.sum(scaled * grad, axis=0, keepdims=True)
    align_ref[...] = jnp.broadcast_to(local[None], align_ref.shape)


def precondition(share, own, other, gradient, out_scale, copies):
    whole = lambda g, s: (0, 0)
    return pl.pallas_call(
        precondition_kernel,
        out_shape=(
            jax.ShapeDtypeStruct((BLOCK, COLS), f32),
            jax.ShapeDtypeStruct((copies, 1, COLS), f32),
        ),
        grid_spec=pltpu.PrefetchScalarGridSpec(
            num_scalar_prefetch=1,
            grid=(1,),
            in_specs=[
                pl.BlockSpec((SHARE, TILE), whole),
                pl.BlockSpec((SHARE, TILE), whole),
                pl.BlockSpec((HALF, COLS), lambda g, s: (s[0], 0)),
                pl.BlockSpec((HALF, COLS), lambda g, s: (1 - s[0], 0)),
                pl.BlockSpec((1, COLS), whole),
            ],
            out_specs=(
                pl.BlockSpec((BLOCK, COLS), whole),
                pl.BlockSpec((copies, 1, COLS), lambda g, s: (0, 0, 0)),
            ),
            scratch_shapes=[
                pltpu.VMEM((BLOCK, 2 * BLOCK), bf16),
                pltpu.VMEM((8, BLOCK), f32),
            ],
        ),
        compiler_params=pltpu.CompilerParams(vmem_limit_bytes=40 * 2**20),
        cost_estimate=pl.CostEstimate(
            flops=2 * 9 * BLOCK * BLOCK * COLS, bytes_accessed=4 * 2**20, transcendentals=0
        ),
        name="precondition",
    )(share, own, other, gradient, gradient, out_scale.reshape(1, COLS))


def clip_kernel(scaled_ref, align_ref, out_ref):
    lanes = jnp.sum(align_ref[...], axis=0)
    alignment = jnp.sum(lanes, axis=1, keepdims=True) * (1.0 / (D * D))
    factor = jnp.minimum(1.0, jnp.sqrt(kl_bound / alignment))
    out_ref[...] = (scaled_ref[...] * factor).astype(bf16)


def clip(scaled, align):
    vmem = pl.BlockSpec(memory_space=pltpu.VMEM)
    return pl.pallas_call(
        clip_kernel,
        out_shape=jax.ShapeDtypeStruct((BLOCK, COLS), bf16),
        in_specs=[vmem, vmem],
        out_specs=vmem,
        compiler_params=pltpu.CompilerParams(vmem_limit_bytes=4 * 2**20),
        cost_estimate=pl.CostEstimate(
            flops=2 * BLOCK * COLS, bytes_accessed=2**20, transcendentals=0
        ),
        name="clip",
    )(scaled, align)


def swap(x, axis):
    return lax.ppermute(x, axis, [(0, 1), (1, 0)])


def cross(x, order):
    pairs = []
    for rank in range(16):
        z4, z2, z1, core = rank >> 3, (rank >> 2) & 1, (rank >> 1) & 1, rank & 1
        if core == order:
            z2 = 1 - z2
        else:
            z4 = 1 - z4
        pairs.append((rank, z4 * 8 + z2 * 4 + z1 * 2 + core))
    return lax.ppermute(x, ("z4", "z2", "z1", "core"), pairs)


def scatter_sum(x, axes, parts):
    pieces = x.reshape(parts, x.shape[0] // parts, x.shape[1])
    return jnp.sum(lax.all_to_all(pieces, axes, 0, 0), axis=0)


def gather(x, axes, parts):
    copies = jnp.broadcast_to(x[None], (parts, *x.shape))
    return lax.all_to_all(copies, axes, 0, 0).reshape(parts * x.shape[0], x.shape[1])


def on_device(activations, gradient, out_scale):
    core = lax.axis_index("core").astype(jnp.int32)
    mine = core.reshape(1)
    theirs = 1 - mine
    away = swap(gram(theirs, activations), "core")
    chip = gram(mine, activations) + away
    part = scatter_sum(chip, ("y", "z1"), 8)
    part = part + cross(part, 0)
    part = part + cross(part, 1)
    own = gather(part, ("y", "z1"), 8)
    other = swap(own, "core")
    scaled, align = precondition(mine, own, other, gradient, out_scale, 32)
    lanes = jnp.sum(lax.all_to_all(align, ("y", "core", "x"), 0, 0), axis=0)
    lanes = jnp.broadcast_to(lanes[None], (16, 1, COLS))
    lanes = lax.all_to_all(lanes, ("z4", "z2", "z1", "z8"), 0, 0)
    return clip(scaled, lanes)


def solution(mesh):
    fine = Mesh(mesh.devices.reshape(SIZES), AXES)
    return jax.shard_map(
        on_device,
        mesh=fine,
        in_specs=(P(DP, MP), P(MP, DP), P(DP)),
        out_specs=P(MP, DP),
        check_vma=False,
    )
```

```python
import functools

import jax
import jax.numpy as jnp
from jax import lax
from jax.experimental import pallas as pl
from jax.experimental.pallas import tpu as pltpu
from jax.sharding import Mesh, PartitionSpec as P

D = 8192
BLOCK = 1024
TILE = 128
HALF = 512
COLS = 128
TOKENS = 65536
DIAGONALS = 16 * TILE
SHARE = DIAGONALS + 64

damping = 0.1
kl_bound = 2.0

AXES = ("y", "z4", "z2", "z1", "core", "x", "z8")
SIZES = (4, 2, 2, 2, 2, 4, 2)
DP = AXES[:5]
MP = AXES[5:]

f32 = jnp.float32
bf16 = jnp.bfloat16


def row_and_column():
    shape = (TILE, TILE)
    return lax.broadcasted_iota(jnp.int32, shape, 0), lax.broadcasted_iota(jnp.int32, shape, 1)


def tile_at(ref, k):
    return ref.at[k * TILE : (k + 1) * TILE, :]


def off_diagonal(i, d):
    return 2 + 3 * i + d - 1


def gram_kernel(share_ref, own_ref, other_ref, out_ref):
    share = share_ref[0]
    row, column = row_and_column()

    def product(lhs, rhs):
        return lax.dot_general(
            lhs, rhs, (((0,), (0,)), ((), ())), preferred_element_type=f32
        )

    own = own_ref[...]
    other = other_ref[...]
    out_ref[DIAGONALS:, :] = jnp.zeros((SHARE - DIAGONALS, TILE), f32)
    for pair in range(2):
        lhs = own[:, pair * 256 : (pair + 1) * 256]
        if pair == 0:
            wide = jnp.concatenate([own, other[:, :256]], axis=1)
        else:
            wide = jnp.concatenate([own[:, 256:], other], axis=1)
        strip = product(lhs, wide)

        def part(i, d):
            return strip[i * TILE : (i + 1) * TILE, (i + d) * TILE : (i + d + 1) * TILE]

        second = part(1, 0)
        tile_at(out_ref, pair)[...] = jnp.where(row <= column, part(0, 0), second)
        out_ref[DIAGONALS + pair : DIAGONALS + pair + 1, :] = jnp.sum(
            jnp.where(row == column, second, 0.0), axis=0, keepdims=True
        )
        for i in range(2):
            for d in range(1, 4):
                tile_at(out_ref, off_diagonal(2 * pair + i, d))[...] = part(i, d)

            @pl.when(share == pair)
            def _():
                tile_at(out_ref, 14 + i)[...] = part(i, 4)


def gram(share, activations):
    tokens = activations.shape[0]
    return pl.pallas_call(
        gram_kernel,
        out_shape=jax.ShapeDtypeStruct((SHARE, TILE), f32),
        grid_spec=pltpu.PrefetchScalarGridSpec(
            num_scalar_prefetch=1,
            grid=(1,),
            in_specs=[
                pl.BlockSpec((tokens, HALF), lambda g, s: (0, s[0])),
                pl.BlockSpec((tokens, HALF), lambda g, s: (0, 1 - s[0])),
            ],
            out_specs=pl.BlockSpec((SHARE, TILE), lambda g, s: (0, 0)),
        ),
        compiler_params=pltpu.CompilerParams(vmem_limit_bytes=24 * 2**20),
        cost_estimate=pl.CostEstimate(
            flops=2 * tokens * 512 * 768, bytes_accessed=3 * 2**20, transcendentals=0
        ),
        name="gram",
    )(share, activations, activations)


def put(factor_ref, sums_ref, tile, i, j):
    high = tile.astype(bf16)
    low = (tile - high.astype(f32)).astype(bf16)
    rows = slice(i * TILE, (i + 1) * TILE)
    factor_ref[rows, j * TILE : (j + 1) * TILE] = high
    factor_ref[rows, BLOCK + j * TILE : BLOCK + (j + 1) * TILE] = low
    part = jnp.abs(tile).reshape(16, 8, TILE)
    sums_ref[:, j * TILE : (j + 1) * TILE] += jnp.sum(part, axis=0)


def unpack(share_ref, packed_ref, factor_ref, sums_ref, base):
    share = share_ref[0]
    row, column = row_and_column()

    def place(k, i, j):
        tile = tile_at(packed_ref, k)[...] * (1.0 / TOKENS)
        put(factor_ref, sums_ref, tile, i, j)
        put(factor_ref, sums_ref, tile.T, j, i)

    def place_diagonal(pair):
        tile = tile_at(packed_ref, pair)[...] * (1.0 / TOKENS)
        turned = tile.T
        diagonal = packed_ref[DIAGONALS + pair : DIAGONALS + pair + 1, :] * (1.0 / TOKENS)
        damped = jnp.where(row == column, damping, 0.0)
        at = base + 2 * pair
        first = jnp.where(row <= column, tile, turned) + damped
        put(factor_ref, sums_ref, first, at, at)
        rest = jnp.where(row > column, tile, turned)
        second = jnp.where(row == column, diagonal, rest) + damped
        put(factor_ref, sums_ref, second, at + 1, at + 1)

    for pair in range(2):
        place_diagonal(pair)
    for i in range(4):
        for d in range(1, 4):
            place(off_diagonal(i, d), base + i, (base + i + d) % 8)
    for core in range(2):

        @pl.when(share == core)
        def _():
            owner = core if base == 0 else 1 - core
            for i in range(2):
                first = base + 2 * owner + i
                place(14 + i, first, (first + 4) % 8)


def unpack_kernel(share_ref, own_ref, factor_ref, sums_ref):
    sums_ref[...] = jnp.zeros_like(sums_ref)
    unpack(share_ref, own_ref, factor_ref, sums_ref, 0)


def unpack_own(share, own):
    vmem = pl.BlockSpec(memory_space=pltpu.VMEM)
    return pl.pallas_call(
        unpack_kernel,
        out_shape=(
            jax.ShapeDtypeStruct((BLOCK, 2 * BLOCK), bf16),
            jax.ShapeDtypeStruct((8, BLOCK), f32),
        ),
        in_specs=[pl.BlockSpec(memory_space=pltpu.SMEM), vmem],
        out_specs=(vmem, vmem),
        compiler_params=pltpu.CompilerParams(vmem_limit_bytes=16 * 2**20),
        cost_estimate=pl.CostEstimate(
            flops=2 * BLOCK * BLOCK, bytes_accessed=5 * 2**20, transcendentals=0
        ),
        name="unpack_own",
    )(share, own)


def precondition_kernel(
    share_ref,
    half_factor_ref,
    own_sums_ref,
    other_ref,
    grad_ref,
    scale_ref,
    factor_ref,
    scaled_ref,
    align_ref,
    sums_ref,
):
    del half_factor_ref
    share = share_ref[0]
    own_rows = pl.ds(pl.multiple_of(share * HALF, HALF), HALF)
    other_rows = pl.ds(pl.multiple_of((1 - share) * HALF, HALF), HALF)
    sums_ref[...] = own_sums_ref[...]
    unpack(share_ref, other_ref, factor_ref, sums_ref, 4)

    bound = 1.0 / jnp.max(jnp.sum(sums_ref[...], axis=0, keepdims=True), axis=1, keepdims=True)
    bound2 = bound * bound

    high = factor_ref[:, :BLOCK]
    low = factor_ref[:, BLOCK:]

    def dot(a, b):
        return jnp.dot(a, b, preferred_element_type=f32)

    def times(v):
        v_high = v.astype(bf16)
        v_low = (v - v_high.astype(f32)).astype(bf16)
        both = dot(jnp.concatenate([v_high, v_low], axis=0), high)
        return both[:COLS] + (both[COLS:] + dot(v_high, low))

    grad = jnp.concatenate([grad_ref[own_rows, :], grad_ref[other_rows, :]], axis=0).astype(f32)
    turned = grad.T
    turned16 = turned.astype(bf16)
    u = 2.0 * bound * turned - bound2 * (dot(turned16, high) + dot(turned16, low))
    v = times(u)
    applied = 2.0 * u - (2.0 * bound * v - bound2 * times(v))
    scaled = applied.T * scale_ref[...]
    scaled_ref[own_rows, :] = scaled[:HALF]
    scaled_ref[other_rows, :] = scaled[HALF:]
    local = jnp.sum(scaled * grad, axis=0, keepdims=True)
    align_ref[...] = jnp.broadcast_to(local[None], align_ref.shape)


def precondition(share, half_factor, own_sums, other, gradient, out_scale, copies):
    vmem = pl.BlockSpec(memory_space=pltpu.VMEM)
    outputs = pl.pallas_call(
        precondition_kernel,
        out_shape=(
            jax.ShapeDtypeStruct((BLOCK, 2 * BLOCK), bf16),
            jax.ShapeDtypeStruct((BLOCK, COLS), f32),
            jax.ShapeDtypeStruct((copies, 1, COLS), f32),
        ),
        in_specs=[pl.BlockSpec(memory_space=pltpu.SMEM)] + [vmem] * 5,
        out_specs=(vmem, vmem, vmem),
        scratch_shapes=[pltpu.VMEM((8, BLOCK), f32)],
        input_output_aliases={1: 0},
        compiler_params=pltpu.CompilerParams(vmem_limit_bytes=24 * 2**20),
        cost_estimate=pl.CostEstimate(
            flops=2 * 9 * BLOCK * BLOCK * COLS, bytes_accessed=4 * 2**20, transcendentals=0
        ),
        name="precondition",
    )(share, half_factor, own_sums, other, gradient, out_scale.reshape(1, COLS))
    return outputs[1:]


def clip_kernel(scaled_ref, align_ref, out_ref):
    lanes = jnp.sum(align_ref[...], axis=0)
    alignment = jnp.sum(lanes, axis=1, keepdims=True) * (1.0 / (D * D))
    factor = jnp.minimum(1.0, jnp.sqrt(kl_bound / alignment))
    out_ref[...] = (scaled_ref[...] * factor).astype(bf16)


def clip(scaled, align):
    vmem = pl.BlockSpec(memory_space=pltpu.VMEM)
    return pl.pallas_call(
        clip_kernel,
        out_shape=jax.ShapeDtypeStruct((BLOCK, COLS), bf16),
        in_specs=[vmem, vmem],
        out_specs=vmem,
        compiler_params=pltpu.CompilerParams(vmem_limit_bytes=4 * 2**20),
        cost_estimate=pl.CostEstimate(
            flops=2 * BLOCK * COLS, bytes_accessed=2**20, transcendentals=0
        ),
        name="clip",
    )(scaled, align)


def swap(x, axis):
    return lax.ppermute(x, axis, [(0, 1), (1, 0)])


def cross(x, order):
    pairs = []
    for rank in range(16):
        z4, z2, z1, core = rank >> 3, (rank >> 2) & 1, (rank >> 1) & 1, rank & 1
        if core == order:
            z2 = 1 - z2
        else:
            z4 = 1 - z4
        pairs.append((rank, z4 * 8 + z2 * 4 + z1 * 2 + core))
    return lax.ppermute(x, ("z4", "z2", "z1", "core"), pairs)


def scatter_sum(x, axes, parts):
    pieces = x.reshape(parts, x.shape[0] // parts, x.shape[1])
    return jnp.sum(lax.all_to_all(pieces, axes, 0, 0), axis=0)


def gather(x, axes, parts):
    copies = jnp.broadcast_to(x[None], (parts, *x.shape))
    return lax.all_to_all(copies, axes, 0, 0).reshape(parts * x.shape[0], x.shape[1])


def on_device(activations, gradient, out_scale):
    core = lax.axis_index("core").astype(jnp.int32)
    mine = core.reshape(1)
    theirs = 1 - mine
    away = swap(gram(theirs, activations), "core")
    chip = gram(mine, activations) + away
    part = scatter_sum(chip, ("z1", "y"), 8)
    part = part + cross(part, 0)
    part = part + cross(part, 1)
    own = gather(part, ("z1", "y"), 8)
    other = swap(own, "core")
    half_factor, own_sums = unpack_own(mine, own)
    scaled, align = precondition(mine, half_factor, own_sums, other, gradient, out_scale, 32)
    lanes = jnp.sum(lax.all_to_all(align, ("y", "core", "x"), 0, 0), axis=0)
    lanes = jnp.broadcast_to(lanes[None], (16, 1, COLS))
    lanes = lax.all_to_all(lanes, ("z4", "z2", "z1", "z8"), 0, 0)
    return clip(scaled, lanes)


def solution(mesh):
    fine = Mesh(mesh.devices.reshape(SIZES), AXES)
    return jax.shard_map(
        on_device,
        mesh=fine,
        in_specs=(P(DP, MP), P(MP, DP), P(DP)),
        out_specs=P(MP, DP),
        check_vma=False,
    )
```

```python
import functools

import jax
import jax.numpy as jnp
from jax import lax
from jax.experimental import pallas as pl
from jax.experimental.pallas import tpu as pltpu
from jax.sharding import Mesh, PartitionSpec as P

D = 8192
BLOCK = 1024
TILE = 128
HALF = 512
COLS = 128
TOKENS = 65536
DIAGONALS = 16 * TILE
SHARE = DIAGONALS + 64

damping = 0.1
kl_bound = 2.0

AXES = ("y", "z4", "z2", "z1", "core", "x", "z8")
SIZES = (4, 2, 2, 2, 2, 4, 2)
DP = AXES[:5]
MP = AXES[5:]

f32 = jnp.float32
bf16 = jnp.bfloat16


def row_and_column():
    shape = (TILE, TILE)
    return lax.broadcasted_iota(jnp.int32, shape, 0), lax.broadcasted_iota(jnp.int32, shape, 1)


def tile_at(ref, k):
    return ref.at[k * TILE : (k + 1) * TILE, :]


def off_diagonal(i, d):
    return 2 + 3 * i + d - 1


def gram_kernel(share_ref, activations_ref, out_ref):
    share = share_ref[0]
    row, column = row_and_column()

    def product(lhs, rhs):
        return lax.dot_general(
            lhs, rhs, (((0,), (0,)), ((), ())), preferred_element_type=f32
        )

    own = activations_ref[:, pl.ds(pl.multiple_of(share * HALF, HALF), HALF)]
    other = activations_ref[:, pl.ds(pl.multiple_of((1 - share) * HALF, HALF), HALF)]
    out_ref[DIAGONALS:, :] = jnp.zeros((SHARE - DIAGONALS, TILE), f32)
    for pair in range(2):
        lhs = own[:, pair * 256 : (pair + 1) * 256]
        if pair == 0:
            wide = jnp.concatenate([own, other[:, :256]], axis=1)
        else:
            wide = jnp.concatenate([own[:, 256:], other], axis=1)
        strip = product(lhs, wide)

        def part(i, d):
            return strip[i * TILE : (i + 1) * TILE, (i + d) * TILE : (i + d + 1) * TILE]

        second = part(1, 0)
        tile_at(out_ref, pair)[...] = jnp.where(row <= column, part(0, 0), second)
        out_ref[DIAGONALS + pair : DIAGONALS + pair + 1, :] = jnp.sum(
            jnp.where(row == column, second, 0.0), axis=0, keepdims=True
        )
        for i in range(2):
            for d in range(1, 4):
                tile_at(out_ref, off_diagonal(2 * pair + i, d))[...] = part(i, d)

            @pl.when(share == pair)
            def _():
                tile_at(out_ref, 14 + i)[...] = part(i, 4)


def gram(share, activations):
    tokens = activations.shape[0]
    return pl.pallas_call(
        gram_kernel,
        out_shape=jax.ShapeDtypeStruct((SHARE, TILE), f32),
        in_specs=[
            pl.BlockSpec(memory_space=pltpu.SMEM),
            pl.BlockSpec(memory_space=pltpu.VMEM),
        ],
        out_specs=pl.BlockSpec(memory_space=pltpu.VMEM),
        compiler_params=pltpu.CompilerParams(vmem_limit_bytes=24 * 2**20),
        cost_estimate=pl.CostEstimate(
            flops=2 * tokens * 512 * 768, bytes_accessed=3 * 2**20, transcendentals=0
        ),
        name="gram",
    )(share, activations)


def put(factor_ref, sums_ref, tile, i, j):
    high = tile.astype(bf16)
    low = (tile - high.astype(f32)).astype(bf16)
    rows = slice(i * TILE, (i + 1) * TILE)
    factor_ref[rows, j * TILE : (j + 1) * TILE] = high
    factor_ref[rows, BLOCK + j * TILE : BLOCK + (j + 1) * TILE] = low
    part = jnp.abs(tile).reshape(16, 8, TILE)
    sums_ref[:, j * TILE : (j + 1) * TILE] += jnp.sum(part, axis=0)


def unpack(share_ref, packed_ref, factor_ref, sums_ref, base):
    share = share_ref[0]
    row, column = row_and_column()

    def place(k, i, j):
        tile = tile_at(packed_ref, k)[...] * (1.0 / TOKENS)
        put(factor_ref, sums_ref, tile, i, j)
        put(factor_ref, sums_ref, tile.T, j, i)

    def place_diagonal(pair):
        tile = tile_at(packed_ref, pair)[...] * (1.0 / TOKENS)
        turned = tile.T
        diagonal = packed_ref[DIAGONALS + pair : DIAGONALS + pair + 1, :] * (1.0 / TOKENS)
        damped = jnp.where(row == column, damping, 0.0)
        at = base + 2 * pair
        first = jnp.where(row <= column, tile, turned) + damped
        put(factor_ref, sums_ref, first, at, at)
        rest = jnp.where(row > column, tile, turned)
        second = jnp.where(row == column, diagonal, rest) + damped
        put(factor_ref, sums_ref, second, at + 1, at + 1)

    for pair in range(2):
        place_diagonal(pair)
    for i in range(4):
        for d in range(1, 4):
            place(off_diagonal(i, d), base + i, (base + i + d) % 8)
    for core in range(2):

        @pl.when(share == core)
        def _():
            owner = core if base == 0 else 1 - core
            for i in range(2):
                first = base + 2 * owner + i
                place(14 + i, first, (first + 4) % 8)


def unpack_kernel(share_ref, own_ref, factor_ref, sums_ref):
    sums_ref[...] = jnp.zeros_like(sums_ref)
    unpack(share_ref, own_ref, factor_ref, sums_ref, 0)


def unpack_own(share, own):
    vmem = pl.BlockSpec(memory_space=pltpu.VMEM)
    return pl.pallas_call(
        unpack_kernel,
        out_shape=(
            jax.ShapeDtypeStruct((BLOCK, 2 * BLOCK), bf16),
            jax.ShapeDtypeStruct((8, BLOCK), f32),
        ),
        in_specs=[pl.BlockSpec(memory_space=pltpu.SMEM), vmem],
        out_specs=(vmem, vmem),
        compiler_params=pltpu.CompilerParams(vmem_limit_bytes=16 * 2**20),
        cost_estimate=pl.CostEstimate(
            flops=2 * BLOCK * BLOCK, bytes_accessed=5 * 2**20, transcendentals=0
        ),
        name="unpack_own",
    )(share, own)


def precondition_kernel(
    share_ref,
    half_factor_ref,
    own_sums_ref,
    other_ref,
    grad_ref,
    scale_ref,
    factor_ref,
    scaled_ref,
    align_ref,
    sums_ref,
):
    del half_factor_ref
    share = share_ref[0]
    own_rows = pl.ds(pl.multiple_of(share * HALF, HALF), HALF)
    other_rows = pl.ds(pl.multiple_of((1 - share) * HALF, HALF), HALF)
    sums_ref[...] = own_sums_ref[...]
    unpack(share_ref, other_ref, factor_ref, sums_ref, 4)

    bound = 1.0 / jnp.max(jnp.sum(sums_ref[...], axis=0, keepdims=True), axis=1, keepdims=True)
    bound2 = bound * bound

    high = factor_ref[:, :BLOCK]
    low = factor_ref[:, BLOCK:]

    def dot(a, b):
        return jnp.dot(a, b, preferred_element_type=f32)

    def times(v):
        v_high = v.astype(bf16)
        v_low = (v - v_high.astype(f32)).astype(bf16)
        both = dot(jnp.concatenate([v_high, v_low], axis=0), high)
        return both[:COLS] + (both[COLS:] + dot(v_high, low))

    grad = jnp.concatenate([grad_ref[own_rows, :], grad_ref[other_rows, :]], axis=0).astype(f32)
    turned = grad.T
    turned16 = turned.astype(bf16)
    u = 2.0 * bound * turned - bound2 * (dot(turned16, high) + dot(turned16, low))
    v = times(u)
    applied = 2.0 * u - (2.0 * bound * v - bound2 * times(v))
    scaled = applied.T * scale_ref[...]
    scaled_ref[own_rows, :] = scaled[:HALF]
    scaled_ref[other_rows, :] = scaled[HALF:]
    local = jnp.sum(scaled * grad, axis=0, keepdims=True)
    align_ref[...] = jnp.broadcast_to(local[None], align_ref.shape)


def precondition(share, half_factor, own_sums, other, gradient, out_scale, copies):
    vmem = pl.BlockSpec(memory_space=pltpu.VMEM)
    outputs = pl.pallas_call(
        precondition_kernel,
        out_shape=(
            jax.ShapeDtypeStruct((BLOCK, 2 * BLOCK), bf16),
            jax.ShapeDtypeStruct((BLOCK, COLS), f32),
            jax.ShapeDtypeStruct((copies, 1, COLS), f32),
        ),
        in_specs=[pl.BlockSpec(memory_space=pltpu.SMEM)] + [vmem] * 5,
        out_specs=(vmem, vmem, vmem),
        scratch_shapes=[pltpu.VMEM((8, BLOCK), f32)],
        input_output_aliases={1: 0},
        compiler_params=pltpu.CompilerParams(vmem_limit_bytes=24 * 2**20),
        cost_estimate=pl.CostEstimate(
            flops=2 * 9 * BLOCK * BLOCK * COLS, bytes_accessed=4 * 2**20, transcendentals=0
        ),
        name="precondition",
    )(share, half_factor, own_sums, other, gradient, out_scale.reshape(1, COLS))
    return outputs[1:]


def clip_kernel(scaled_ref, align_ref, out_ref):
    lanes = jnp.sum(align_ref[...], axis=0)
    alignment = jnp.sum(lanes, axis=1, keepdims=True) * (1.0 / (D * D))
    factor = jnp.minimum(1.0, jnp.sqrt(kl_bound / alignment))
    out_ref[...] = (scaled_ref[...] * factor).astype(bf16)


def clip(scaled, align):
    vmem = pl.BlockSpec(memory_space=pltpu.VMEM)
    return pl.pallas_call(
        clip_kernel,
        out_shape=jax.ShapeDtypeStruct((BLOCK, COLS), bf16),
        in_specs=[vmem, vmem],
        out_specs=vmem,
        compiler_params=pltpu.CompilerParams(vmem_limit_bytes=4 * 2**20),
        cost_estimate=pl.CostEstimate(
            flops=2 * BLOCK * COLS, bytes_accessed=2**20, transcendentals=0
        ),
        name="clip",
    )(scaled, align)


def swap(x, axis):
    return lax.ppermute(x, axis, [(0, 1), (1, 0)])


def cross(x, order):
    pairs = []
    for rank in range(16):
        z4, z2, z1, core = rank >> 3, (rank >> 2) & 1, (rank >> 1) & 1, rank & 1
        if core == order:
            z2 = 1 - z2
        else:
            z4 = 1 - z4
        pairs.append((rank, z4 * 8 + z2 * 4 + z1 * 2 + core))
    return lax.ppermute(x, ("z4", "z2", "z1", "core"), pairs)


def scatter_sum(x, axes, parts):
    pieces = x.reshape(parts, x.shape[0] // parts, x.shape[1])
    return jnp.sum(lax.all_to_all(pieces, axes, 0, 0), axis=0)


def gather(x, axes, parts):
    copies = jnp.broadcast_to(x[None], (parts, *x.shape))
    return lax.all_to_all(copies, axes, 0, 0).reshape(parts * x.shape[0], x.shape[1])


def on_device(activations, gradient, out_scale):
    core = lax.axis_index("core").astype(jnp.int32)
    mine = core.reshape(1)
    theirs = 1 - mine
    away = swap(gram(theirs, activations), "core")
    chip = gram(mine, activations) + away
    part = scatter_sum(chip, ("z1", "y"), 8)
    part = part + cross(part, 0)
    part = part + cross(part, 1)
    own = gather(part, ("z1", "y"), 8)
    other = swap(own, "core")
    half_factor, own_sums = unpack_own(mine, own)
    scaled, align = precondition(mine, half_factor, own_sums, other, gradient, out_scale, 32)
    lanes = jnp.sum(lax.all_to_all(align, ("y", "core", "x"), 0, 0), axis=0)
    lanes = jnp.broadcast_to(lanes[None], (16, 1, COLS))
    lanes = lax.all_to_all(lanes, ("z4", "z2", "z1", "z8"), 0, 0)
    return clip(scaled, lanes)


def solution(mesh):
    fine = Mesh(mesh.devices.reshape(SIZES), AXES)
    return jax.shard_map(
        on_device,
        mesh=fine,
        in_specs=(P(DP, MP), P(MP, DP), P(DP)),
        out_specs=P(MP, DP),
        check_vma=False,
    )
```

```python
import functools

import jax
import jax.numpy as jnp
from jax import lax
from jax.experimental import pallas as pl
from jax.experimental.pallas import tpu as pltpu
from jax.sharding import Mesh, PartitionSpec as P

D = 8192
BLOCK = 1024
TILE = 128
HALF = 512
COLS = 128
TOKENS = 65536
DIAGONALS = 16 * TILE
SHARE = DIAGONALS + 64

damping = 0.1
kl_bound = 2.0

AXES = ("y2", "y1", "z4", "z2", "z1", "core", "x", "z8")
SIZES = (2, 2, 2, 2, 2, 2, 4, 2)
DP = AXES[:6]
MP = AXES[6:]

f32 = jnp.float32
bf16 = jnp.bfloat16


def row_and_column():
    shape = (TILE, TILE)
    return lax.broadcasted_iota(jnp.int32, shape, 0), lax.broadcasted_iota(jnp.int32, shape, 1)


def tile_at(ref, k):
    return ref.at[k * TILE : (k + 1) * TILE, :]


def off_diagonal(i, d):
    return 2 + 3 * i + d - 1


def gram_kernel(share_ref, own_ref, other_ref, out_ref):
    share = share_ref[0]
    row, column = row_and_column()

    def product(lhs, rhs):
        return lax.dot_general(
            lhs, rhs, (((0,), (0,)), ((), ())), preferred_element_type=f32
        )

    own = own_ref[...]
    other = other_ref[...]
    out_ref[DIAGONALS:, :] = jnp.zeros((SHARE - DIAGONALS, TILE), f32)
    for pair in range(2):
        lhs = own[:, pair * 256 : (pair + 1) * 256]
        if pair == 0:
            wide = jnp.concatenate([own, other[:, :256]], axis=1)
        else:
            wide = jnp.concatenate([own[:, 256:], other], axis=1)
        strip = product(lhs, wide)

        def part(i, d):
            return strip[i * TILE : (i + 1) * TILE, (i + d) * TILE : (i + d + 1) * TILE]

        second = part(1, 0)
        tile_at(out_ref, pair)[...] = jnp.where(row <= column, part(0, 0), second)
        out_ref[DIAGONALS + pair : DIAGONALS + pair + 1, :] = jnp.sum(
            jnp.where(row == column, second, 0.0), axis=0, keepdims=True
        )
        for i in range(2):
            for d in range(1, 4):
                tile_at(out_ref, off_diagonal(2 * pair + i, d))[...] = part(i, d)

            @pl.when(share == pair)
            def _():
                tile_at(out_ref, 14 + i)[...] = part(i, 4)


def gram(share, activations):
    tokens = activations.shape[0]
    return pl.pallas_call(
        gram_kernel,
        out_shape=jax.ShapeDtypeStruct((SHARE, TILE), f32),
        grid_spec=pltpu.PrefetchScalarGridSpec(
            num_scalar_prefetch=1,
            grid=(1,),
            in_specs=[
                pl.BlockSpec((tokens, HALF), lambda g, s: (0, s[0])),
                pl.BlockSpec((tokens, HALF), lambda g, s: (0, 1 - s[0])),
            ],
            out_specs=pl.BlockSpec((SHARE, TILE), lambda g, s: (0, 0)),
        ),
        compiler_params=pltpu.CompilerParams(vmem_limit_bytes=24 * 2**20),
        cost_estimate=pl.CostEstimate(
            flops=2 * tokens * 512 * 768, bytes_accessed=3 * 2**20, transcendentals=0
        ),
        name="gram",
    )(share, activations, activations)


def put(factor_ref, sums_ref, tile, i, j):
    high = tile.astype(bf16)
    low = (tile - high.astype(f32)).astype(bf16)
    rows = slice(i * TILE, (i + 1) * TILE)
    factor_ref[rows, j * TILE : (j + 1) * TILE] = high
    factor_ref[rows, BLOCK + j * TILE : BLOCK + (j + 1) * TILE] = low
    part = jnp.abs(tile).reshape(16, 8, TILE)
    sums_ref[:, j * TILE : (j + 1) * TILE] += jnp.sum(part, axis=0)


def unpack(share_ref, packed_ref, factor_ref, sums_ref, base):
    share = share_ref[0]
    row, column = row_and_column()

    def place(k, i, j):
        tile = tile_at(packed_ref, k)[...] * (1.0 / TOKENS)
        put(factor_ref, sums_ref, tile, i, j)
        put(factor_ref, sums_ref, tile.T, j, i)

    def place_diagonal(pair):
        tile = tile_at(packed_ref, pair)[...] * (1.0 / TOKENS)
        turned = tile.T
        diagonal = packed_ref[DIAGONALS + pair : DIAGONALS + pair + 1, :] * (1.0 / TOKENS)
        damped = jnp.where(row == column, damping, 0.0)
        at = base + 2 * pair
        first = jnp.where(row <= column, tile, turned) + damped
        put(factor_ref, sums_ref, first, at, at)
        rest = jnp.where(row > column, tile, turned)
        second = jnp.where(row == column, diagonal, rest) + damped
        put(factor_ref, sums_ref, second, at + 1, at + 1)

    for pair in range(2):
        place_diagonal(pair)
    for i in range(4):
        for d in range(1, 4):
            place(off_diagonal(i, d), base + i, (base + i + d) % 8)
    for core in range(2):

        @pl.when(share == core)
        def _():
            owner = core if base == 0 else 1 - core
            for i in range(2):
                first = base + 2 * owner + i
                place(14 + i, first, (first + 4) % 8)


def unpack_kernel(share_ref, own_ref, factor_ref, sums_ref):
    sums_ref[...] = jnp.zeros_like(sums_ref)
    unpack(share_ref, own_ref, factor_ref, sums_ref, 0)


def unpack_own(share, own):
    vmem = pl.BlockSpec(memory_space=pltpu.VMEM)
    return pl.pallas_call(
        unpack_kernel,
        out_shape=(
            jax.ShapeDtypeStruct((BLOCK, 2 * BLOCK), bf16),
            jax.ShapeDtypeStruct((8, BLOCK), f32),
        ),
        in_specs=[pl.BlockSpec(memory_space=pltpu.SMEM), vmem],
        out_specs=(vmem, vmem),
        compiler_params=pltpu.CompilerParams(vmem_limit_bytes=16 * 2**20),
        cost_estimate=pl.CostEstimate(
            flops=2 * BLOCK * BLOCK, bytes_accessed=5 * 2**20, transcendentals=0
        ),
        name="unpack_own",
    )(share, own)


def precondition_kernel(
    share_ref,
    half_factor_ref,
    own_sums_ref,
    other_ref,
    grad_ref,
    scale_ref,
    factor_ref,
    scaled_ref,
    align_ref,
    sums_ref,
):
    del half_factor_ref
    share = share_ref[0]
    own_rows = pl.ds(pl.multiple_of(share * HALF, HALF), HALF)
    other_rows = pl.ds(pl.multiple_of((1 - share) * HALF, HALF), HALF)
    sums_ref[...] = own_sums_ref[...]
    unpack(share_ref, other_ref, factor_ref, sums_ref, 4)

    bound = 1.0 / jnp.max(jnp.sum(sums_ref[...], axis=0, keepdims=True), axis=1, keepdims=True)
    bound2 = bound * bound

    high = factor_ref[:, :BLOCK]
    low = factor_ref[:, BLOCK:]

    def dot(a, b):
        return jnp.dot(a, b, preferred_element_type=f32)

    def times(v):
        v_high = v.astype(bf16)
        v_low = (v - v_high.astype(f32)).astype(bf16)
        both = dot(jnp.concatenate([v_high, v_low], axis=0), high)
        return both[:COLS] + (both[COLS:] + dot(v_high, low))

    grad = jnp.concatenate([grad_ref[own_rows, :], grad_ref[other_rows, :]], axis=0).astype(f32)
    turned = grad.T
    turned16 = turned.astype(bf16)
    u = 2.0 * bound * turned - bound2 * (dot(turned16, high) + dot(turned16, low))
    v = times(u)
    applied = 2.0 * u - (2.0 * bound * v - bound2 * times(v))
    scaled = applied.T * scale_ref[...]
    scaled_ref[own_rows, :] = scaled[:HALF]
    scaled_ref[other_rows, :] = scaled[HALF:]
    local = jnp.sum(scaled * grad, axis=0, keepdims=True)
    align_ref[...] = jnp.broadcast_to(local[None], align_ref.shape)


def precondition(share, half_factor, own_sums, other, gradient, out_scale, copies):
    vmem = pl.BlockSpec(memory_space=pltpu.VMEM)
    outputs = pl.pallas_call(
        precondition_kernel,
        out_shape=(
            jax.ShapeDtypeStruct((BLOCK, 2 * BLOCK), bf16),
            jax.ShapeDtypeStruct((BLOCK, COLS), f32),
            jax.ShapeDtypeStruct((copies, 1, COLS), f32),
        ),
        in_specs=[pl.BlockSpec(memory_space=pltpu.SMEM)] + [vmem] * 5,
        out_specs=(vmem, vmem, vmem),
        scratch_shapes=[pltpu.VMEM((8, BLOCK), f32)],
        input_output_aliases={1: 0},
        compiler_params=pltpu.CompilerParams(vmem_limit_bytes=24 * 2**20),
        cost_estimate=pl.CostEstimate(
            flops=2 * 9 * BLOCK * BLOCK * COLS, bytes_accessed=4 * 2**20, transcendentals=0
        ),
        name="precondition",
    )(share, half_factor, own_sums, other, gradient, out_scale.reshape(1, COLS))
    return outputs[1:]


def clip_kernel(scaled_ref, align_ref, out_ref):
    lanes = jnp.sum(align_ref[...], axis=0)
    alignment = jnp.sum(lanes, axis=1, keepdims=True) * (1.0 / (D * D))
    factor = jnp.minimum(1.0, jnp.sqrt(kl_bound / alignment))
    out_ref[...] = (scaled_ref[...] * factor).astype(bf16)


def clip(scaled, align):
    vmem = pl.BlockSpec(memory_space=pltpu.VMEM)
    return pl.pallas_call(
        clip_kernel,
        out_shape=jax.ShapeDtypeStruct((BLOCK, COLS), bf16),
        in_specs=[vmem, vmem],
        out_specs=vmem,
        compiler_params=pltpu.CompilerParams(vmem_limit_bytes=4 * 2**20),
        cost_estimate=pl.CostEstimate(
            flops=2 * BLOCK * COLS, bytes_accessed=2**20, transcendentals=0
        ),
        name="clip",
    )(scaled, align)


def swap(x, axis):
    return lax.ppermute(x, axis, [(0, 1), (1, 0)])


def cross(x, order):
    pairs = []
    for rank in range(16):
        z4, z2, z1, core = rank >> 3, (rank >> 2) & 1, (rank >> 1) & 1, rank & 1
        if core == order:
            z2 = 1 - z2
        else:
            z4 = 1 - z4
        pairs.append((rank, z4 * 8 + z2 * 4 + z1 * 2 + core))
    return lax.ppermute(x, ("z4", "z2", "z1", "core"), pairs)


def scatter_sum(x, axes, parts):
    pieces = x.reshape(parts, x.shape[0] // parts, x.shape[1])
    return jnp.sum(lax.all_to_all(pieces, axes, 0, 0), axis=0)


def gather(x, axes, parts):
    copies = jnp.broadcast_to(x[None], (parts, *x.shape))
    return lax.all_to_all(copies, axes, 0, 0).reshape(parts * x.shape[0], x.shape[1])


def on_device(activations, gradient, out_scale):
    core = lax.axis_index("core").astype(jnp.int32)
    mine = core.reshape(1)
    theirs = 1 - mine
    away = swap(gram(theirs, activations), "core")
    chip = gram(mine, activations) + away
    part = scatter_sum(chip, ("y2", "z1", "y1"), 8)
    part = part + cross(part, 0)
    part = part + cross(part, 1)
    own = gather(part, ("y2", "z1", "y1"), 8)
    other = swap(own, "core")
    half_factor, own_sums = unpack_own(mine, own)
    scaled, align = precondition(mine, half_factor, own_sums, other, gradient, out_scale, 32)
    lanes = jnp.sum(lax.all_to_all(align, ("y2", "y1", "core", "x"), 0, 0), axis=0)
    lanes = jnp.broadcast_to(lanes[None], (16, 1, COLS))
    lanes = lax.all_to_all(lanes, ("z4", "z2", "z1", "z8"), 0, 0)
    return clip(scaled, lanes)


def solution(mesh):
    fine = Mesh(mesh.devices.reshape(SIZES), AXES)
    return jax.shard_map(
        on_device,
        mesh=fine,
        in_specs=(P(DP, MP), P(MP, DP), P(DP)),
        out_specs=P(MP, DP),
        check_vma=False,
    )
```
